1024 devices in a mesh: member: 16 (over x, z_hi), shard: 64 (over y, z_lo, core).
Axes of the slice: x: 4, y: 8, z: 16 (z_hi: 4, z_lo: 4; z = z_hi * 4 + z_lo), core: 2. Of those that a mesh axis runs over, the one named last changes fastest.
Arguments:
- trunk_out: bfloat16 [128, 8192], P('shard', 'member'), may hold values from -6 to 6
- segment_ids: int32 [128], replicated, may hold values from 0 to 7, never falling along the last dimension, each value on 1 to 32 neighbouring positions
- pair_order: int32 [8], replicated, may hold values from 0 to 7, each once
- w_query: bfloat16 [16, 64, 4096, 128], P('member', 'shard'), may hold values from -0.25 to 0.25
- w_key_value: bfloat16 [16, 64, 512, 256], P('member', 'shard'), may hold values from -0.0625 to 0.0625
- w_out: bfloat16 [16, 4096, 8192], P('member', 'shard'), may hold values from -0.09375 to 0.09375
- norm_gain: float32 [16, 8192], P('member'), may hold values from 0.1 to 1.9
- reward_weight: float32 [16, 8192], P('member'), may hold values from -0.0625 to 0.0625
Outputs:
- trunk_grad: float32 [128, 8192], P('member', 'shard')
- rewards: float32 [16, 8], P('member')
The draws below stay inside these ranges and needn't reach their ends.
Inputs may be any that keep to these rules, and one draw needn't show every extreme that they name: `segment_ids`: segment numbers never fall along the tokens; every sequence 0 to 7 has 1 to 32 tokens, and one has exactly 32. Each sequence appears once; sequence pair_order[2 * i] is preferred to sequence pair_order[2 * i + 1].
All inputs are finite; a program needn't handle non-finite values.
Results may differ from the reference program's by a relative error of at most 0.011.
Values may be sent and summed in bfloat16 or wider, within the bound.
A program may use at most 32 MiB of HBM per device.

```python
import math
import jax
import jax.numpy as jnp
import numpy as np
from jax import lax

D = 8192
HD = 128
TOK = 128
SEG_MOST = 32
HEADS = 32
KVH = 4
QG = 8
SEQS = 8
MEMBERS = 16


def steps_of(own_key, dims, shards, least, largest):
    def one(position, parts):
        steps = jax.random.uniform(jax.random.fold_in(jax.random.fold_in(own_key, 6), position), (parts,), jnp.float32, least / len(shards), largest / len(shards))
        return jnp.repeat(jnp.exp(steps), dims[position] // parts).reshape((-1,) + (1,) * (len(dims) - position - 1))

    factor_of = one(*shards[0])
    for cut in shards[1:]:
        factor_of = factor_of * one(*cut)
    return factor_of


def profile(count, total, bound, lean):
    portions = [(1 << 20) // math.isqrt(standing ** lean) + 1 for standing in range(2, count + 1)]
    rest, holding = total - bound - (count - 1), [1] * (count - 1)
    while rest > 0:
        free = [i for i in range(count - 1) if holding[i] < bound]
        pool, left = sum([portions[i] for i in free]), rest
        for i in free:
            addition = min(bound - holding[i], max(1, left * portions[i] // pool), rest)
            holding[i] = holding[i] + addition
            rest = rest - addition
    return np.array([bound] + holding)


def ragged_sizes(rng, amount, total, bound, lean):
    if amount == 2:
        one = jax.random.randint(rng, (), max(1, total - bound), min(bound, total - 1) + 1)
        return jnp.stack([one, total - one])
    sizes = jnp.asarray(profile(amount, total, bound, lean), jnp.int32)
    twos = (amount - 1) // 2
    giver, receiver = sizes[1:1 + 2 * twos:2], sizes[2:2 + 2 * twos:2]
    room = jnp.minimum(giver - 1, bound - receiver)
    passed = jax.random.randint(jax.random.fold_in(rng, 1), (twos,), 0, 1 << 20) % (room + 1)
    sizes = sizes.at[1:1 + 2 * twos:2].set(giver - passed).at[2:2 + 2 * twos:2].set(receiver + passed)
    return sizes[jax.random.permutation(jax.random.fold_in(rng, 2), amount)]


def centred(own_key, shape, deviation, limit, cuts=(), held_as=jnp.bfloat16):
    values = deviation * jax.random.normal(own_key, shape, jnp.float32)
    if cuts:
        values = values * steps_of(own_key, shape, cuts, -0.22, 0.18)
    return jnp.clip(values, -limit, limit).astype(held_as)


def setup_inputs(seed: int = 0) -> dict:
    seeds = jax.random.split(jax.random.key(seed), 9)
    trunk_out = centred(seeds[0], (TOK, D), 1.0, 6.0, ((0, 64), (1, 16)))
    segment_ids = jnp.searchsorted(jnp.cumsum(ragged_sizes(seeds[1], SEQS, TOK, SEG_MOST, 1)), jnp.arange(TOK), side="right").astype(jnp.int32)
    pair_order = jax.random.permutation(seeds[2], SEQS).astype(jnp.int32)
    w_query = centred(seeds[3], (MEMBERS, 2 * HEADS, D // 2, HD), (D // 16) ** -0.5, 0.25, ((0, 16), (1, 64)))
    w_key_value = centred(seeds[4], (MEMBERS, 2 * HEADS, D // (2 * QG), 2 * HD), D ** -0.5, 0.0625, ((0, 16), (1, 64)))
    w_out = centred(seeds[5], (MEMBERS, HEADS * HD, D), (HEADS * HD) ** -0.5, 0.09375, ((0, 16), (1, 64)))
    norm_gain = jnp.clip(1.0 + 0.18 * jax.random.normal(seeds[6], (MEMBERS, D), jnp.float32), 0.1, 1.9)
    reward_weight = centred(seeds[7], (MEMBERS, D), D ** -0.5, 0.0625, ((0, 16),), jnp.float32)
    return {"trunk_out": trunk_out, "segment_ids": segment_ids, "pair_order": pair_order, "w_query": w_query, "w_key_value": w_key_value, "w_out": w_out, "norm_gain": norm_gain, "reward_weight": reward_weight}


softcap_limit = 20.0
loss_scale = 256.0
norm_eps = 1e-05

def unfold_query(packed):
    return packed.reshape(HEADS, 2, D // 2, HD).transpose(1, 2, 0, 3).reshape(D, HEADS * HD)

def unfold_kv(portion):
    return portion.transpose(2, 1, 3, 0, 4).reshape(D, KVH * HD)

def reference(trunk_out, segment_ids, pair_order, w_query, w_key_value, w_out, norm_gain, reward_weight):
    scale_factor = 1.0 / math.sqrt(HD)
    positions = jnp.arange(TOK)
    allowed = (segment_ids[:, None] == segment_ids[None, :]) & (positions[None, :] <= positions[:, None])
    member_of = jnp.arange(SEQS)[:, None] == segment_ids[None, :]
    pooling = member_of.astype(jnp.bfloat16)
    lengths = lax.optimization_barrier(jnp.sum(member_of.astype(jnp.float32), axis=1))
    pooled_input = jnp.dot(pooling, trunk_out, preferred_element_type=jnp.float32) / lengths[:, None]
    chosen_ids = pair_order[0::2]
    rejected_ids = pair_order[1::2]

    def one_member(carry_sum, member_weights):
        query_packed, kv_packed, out_full, gain_vector, head_weight = member_weights
        query_full = unfold_query(query_packed)
        arranged = kv_packed.reshape(KVH, QG, 2, D // (2 * QG), 2 * HD)
        key_full = unfold_kv(arranged[..., :HD])
        value_full = unfold_kv(arranged[..., HD:])
        queries = jnp.dot(trunk_out, query_full, preferred_element_type=jnp.float32).astype(jnp.bfloat16).reshape(TOK, HEADS, HD)
        keys_all = jnp.dot(trunk_out, key_full, preferred_element_type=jnp.float32).astype(jnp.bfloat16).reshape(TOK, KVH, HD)
        values_all = jnp.dot(trunk_out, value_full, preferred_element_type=jnp.float32).astype(jnp.bfloat16).reshape(TOK, KVH, HD)
        key_heads = jnp.repeat(keys_all, QG, axis=1).astype(jnp.float32)
        value_heads = jnp.repeat(values_all, QG, axis=1).astype(jnp.float32)
        raw_scores = jnp.einsum('thd,shd->hts', queries.astype(jnp.float32), key_heads) * scale_factor
        capped = softcap_limit * jnp.tanh(raw_scores / softcap_limit)
        weights_exp = jnp.where(allowed[None], jnp.exp(capped), 0.0)
        attention = weights_exp / lax.optimization_barrier(jnp.sum(weights_exp, axis=2, keepdims=True))
        attention_low = attention.astype(jnp.bfloat16)
        attended = jnp.einsum('hts,shd->thd', attention_low.astype(jnp.float32), value_heads).astype(jnp.bfloat16).reshape(TOK, HEADS * HD)
        seq_mean = (jnp.dot(pooling, attended, preferred_element_type=jnp.float32) / lengths[:, None]).astype(jnp.bfloat16)
        hidden = pooled_input + jnp.dot(seq_mean, out_full, preferred_element_type=jnp.float32)
        inverse_rms = lax.rsqrt(lax.optimization_barrier(jnp.mean(hidden * hidden, axis=1)) + norm_eps)
        normed = hidden * inverse_rms[:, None] * gain_vector
        rewards = lax.optimization_barrier(jnp.sum(normed * head_weight, axis=1))
        margin = rewards[chosen_ids] - rewards[rejected_ids]
        pair_slope = loss_scale * jax.nn.sigmoid(-margin)
        reward_grad = jnp.zeros((SEQS,), jnp.float32).at[rejected_ids].add(pair_slope).at[chosen_ids].add(-pair_slope)
        scaled_grad = reward_grad[:, None] * head_weight * gain_vector
        hidden_grad = inverse_rms[:, None] * (scaled_grad - hidden * (inverse_rms ** 2)[:, None] * lax.optimization_barrier(jnp.mean(hidden * scaled_grad, axis=1, keepdims=True)))
        per_token = hidden_grad / lengths[:, None]
        mean_grad = jnp.dot(hidden_grad.astype(jnp.bfloat16), out_full.T, preferred_element_type=jnp.float32) / lengths[:, None]
        out_grad = mean_grad[segment_ids].astype(jnp.bfloat16).reshape(TOK, HEADS, HD).astype(jnp.float32)
        prob_grad = jnp.einsum('thd,shd->hts', out_grad, value_heads)
        score_grad = attention * (prob_grad - lax.optimization_barrier(jnp.sum(attention * prob_grad, axis=2, keepdims=True)))
        raw_grad = (score_grad * (1.0 - (capped / softcap_limit) ** 2) * scale_factor).astype(jnp.bfloat16).astype(jnp.float32)
        query_grad = jnp.einsum('hts,shd->thd', raw_grad, key_heads).astype(jnp.bfloat16).reshape(TOK, HEADS * HD)
        key_grad = jnp.einsum('hts,thd->shd', raw_grad, queries.astype(jnp.float32))
        key_grad = key_grad.reshape(TOK, KVH, QG, HD).sum(axis=2).astype(jnp.bfloat16).reshape(TOK, KVH * HD)
        value_grad = jnp.einsum('hts,thd->shd', attention_low.astype(jnp.float32), out_grad)
        value_grad = value_grad.reshape(TOK, KVH, QG, HD).sum(axis=2).astype(jnp.bfloat16).reshape(TOK, KVH * HD)
        member_grad = jnp.dot(query_grad, query_full.T, preferred_element_type=jnp.float32)
        member_grad = member_grad + jnp.dot(key_grad, key_full.T, preferred_element_type=jnp.float32)
        member_grad = member_grad + jnp.dot(value_grad, value_full.T, preferred_element_type=jnp.float32)
        member_grad = member_grad + per_token[segment_ids]
        return (carry_sum + member_grad, rewards)
    trunk_grad, rewards = lax.scan(one_member, jnp.zeros((TOK, D), jnp.float32), (w_query, w_key_value, w_out, norm_gain, reward_weight))
    return (trunk_grad, rewards)
```

```python
import functools
import math
import types

import jax
import jax.numpy as jnp
from jax import lax
from jax.experimental import pallas as pl
from jax.experimental.pallas import tpu as pltpu
from jax.sharding import PartitionSpec as P

MESH = pl.DeviceIdType.MESH
F32 = jnp.float32
BF16 = jnp.bfloat16
SEQS = 8
CAP = 20.0
LOSS_SCALE = 256.0
EPS = 1e-05
ZL = 4


def loop(count, body):
    def step(index, carry):
        body(index)
        return carry

    lax.fori_loop(0, count, step, 0)


def matmul(a, b, contract=((1,), (0,))):
    return lax.dot_general(a, b, (contract, ((), ())), preferred_element_type=F32)


def scratch_list(dims):
    X, ZH, Y = dims
    tok = 16 * Y
    owned = tok // 16
    heads = 4 * Y
    blocks = heads // 4
    rows = 8 * ZH
    dma = pltpu.SemaphoreType.DMA
    return dict(
        wq=pltpu.VMEM((heads * 128, 128), BF16),
        wkv=pltpu.VMEM((heads * 16, 256), BF16),
        wo=pltpu.VMEM((64, heads * 256), BF16),
        gain=pltpu.VMEM((1, heads * 256), F32),
        weight=pltpu.VMEM((1, heads * 256), F32),
        pair_out=pltpu.VMEM((8, 128), F32),
        pair_in=pltpu.VMEM((8, 128), F32),
        z_out=pltpu.VMEM((8, 128), F32),
        z_in=pltpu.VMEM((ZH * ZL, 8, 128), F32),
        own=pltpu.VMEM((ZH, Y, 2, 16, 128), BF16),
        feat=pltpu.VMEM((X, ZH, Y, 2, 16, 128), BF16),
        q_out=pltpu.VMEM((tok, 128), F32),
        q_in=pltpu.VMEM((tok, 128), F32),
        kv_out=pltpu.VMEM((16, 2, owned, 128), F32),
        kv_in=pltpu.VMEM((16, 2, owned, 128), F32),
        kv_all=pltpu.VMEM((16, 2 * owned, 128), BF16),
        head_out=pltpu.VMEM((heads, 8, 128), F32),
        head_in=pltpu.VMEM((heads, 8, 128), F32),
        part_out=pltpu.VMEM((heads, 8, 128), F32),
        part_in=pltpu.VMEM((heads, 8, 128), F32),
        half=pltpu.VMEM((heads, 8, 128), F32),
        hidden=pltpu.VMEM((2, heads, 8, 128), F32),
        dims_out=pltpu.VMEM((8, 128), F32),
        dims_in=pltpu.VMEM((8, 128), F32),
        dkv_out=pltpu.VMEM((16, 2, owned, 128), F32),
        dkv_in=pltpu.VMEM((8, 2, owned, 128), F32),
        dkv_all=pltpu.VMEM((16, 2 * owned, 128), BF16),
        token_out=pltpu.VMEM((2 * heads, 8, 128), F32),
        term=pltpu.VMEM((4, tok, 128), F32),
        x_out=pltpu.VMEM((blocks, X, 2, 2, rows, 128), BF16),
        x_in=pltpu.VMEM((blocks, X, 2, 2, rows, 128), BF16),
        y_out=pltpu.VMEM((blocks, 2, 2, rows, 128), BF16),
        y_in=pltpu.VMEM((Y, ZL, rows, 128), BF16),
        l_out=pltpu.VMEM((ZL * ZH, 8, 128), F32),
        l_in=pltpu.VMEM((ZL * ZH, 8, 128), F32),
        w_sem=dma((5,)),
        pair_s=dma,
        pair_r=dma,
        z_s=dma,
        z_r=dma((ZH,)),
        ya_s=dma,
        ya_r=dma((ZH,)),
        xa_s=dma,
        xa_s0=dma,
        xa_r=dma((X, ZH)),
        q_s=dma,
        q_r=dma,
        kv_s=dma,
        kv_r=dma,
        kva_s=dma,
        kva_r=dma,
        h1_s=dma,
        h1_r=dma,
        h2_s=dma,
        h2_r=dma,
        h3_s=dma,
        h3_r=dma,
        h4_s=dma,
        h4_r=dma,
        d_s=dma,
        d_r=dma,
        dkv_s=dma,
        dkv_r=dma,
        dka_s=dma,
        dka_r=dma,
        ex_s=dma((blocks,)),
        ex_r=dma((blocks,)),
        ey_s=dma((blocks, 2)),
        ey_r=dma((Y,)),
        el_s=dma,
        el_r=dma,
    )


def kernel(
    dims, names, trunk_ref, seg_ref, order_ref, wq_hbm, wkv_hbm, wo_hbm, gain_hbm, weight_hbm, out_ref, reward_ref, *scratch
):
    r = types.SimpleNamespace(**dict(zip(names, scratch)))
    pending = []
    X, ZH, Y = dims
    XH = X // 2
    tok = 16 * Y
    owned = tok // 16
    heads = 4 * Y
    tiles = 2 * heads
    blocks = heads // 4
    rows = 8 * ZH
    kv_tiles = heads // 8
    scale = 1.0 / math.sqrt(128)

    member = lax.axis_index("member")
    shard = lax.axis_index("shard")
    x, zh = member // ZH, member % ZH
    y, zl, c = shard // (2 * ZL), shard % (2 * ZL) // 2, shard % 2
    p = c * ZL + zl
    ybit = y % 2
    group_y = y - ybit
    o = ybit * 8 + p
    block = ybit * ZL + zl
    head = y * ZL + zl
    xs = x % XH
    target_core = x // XH

    def at(x_=x, zh_=zh, y_=y, zl_=zl, c_=c):
        return (x_ * ZH + zh_, (y_ * ZL + zl_) * 2 + c_)

    def send(src, dst, send_sem, recv_sem, device):
        pltpu.make_async_remote_copy(
            src_ref=src, dst_ref=dst, send_sem=send_sem, recv_sem=recv_sem, device_id=device, device_id_type=MESH
        ).start()

    def wait(sem, ref):
        pltpu.make_async_copy(ref, ref, sem).wait()

    def later(sem, ref):
        pending.append(lambda: wait(sem, ref))

    def z_peer(index):
        other = (zh * ZL + zl + 1 + index) % (ZH * ZL)
        return other, at(zh_=other // ZL, zl_=other % ZL)

    def head_peer(index):
        other = (head + 1 + index) % heads
        return other, at(y_=other // ZL, zl_=other % ZL)

    def group_peer(index):
        other = (o + 1 + index) % 16
        q = other % 8
        return other, at(y_=group_y + other // 8, zl_=q % ZL, c_=q // ZL)

    weight_copies = [
        pltpu.make_async_copy(wq_hbm, r.wq, r.w_sem.at[0]),
        pltpu.make_async_copy(wkv_hbm, r.wkv, r.w_sem.at[1]),
        pltpu.make_async_copy(wo_hbm, r.wo, r.w_sem.at[2]),
        pltpu.make_async_copy(gain_hbm, r.gain, r.w_sem.at[3]),
        pltpu.make_async_copy(weight_hbm, r.weight, r.w_sem.at[4]),
    ]
    for copy in weight_copies:
        copy.start()

    barrier = pltpu.get_barrier_semaphore()

    def greet(device):
        pl.semaphore_signal(barrier, inc=1, device_id=device, device_id_type=MESH)

    loop(ZH * ZL - 1, lambda i: greet(z_peer(i)[1]))
    loop(4 * (Y - 1), lambda i: greet(at(y_=(y + 1 + i // ZL) % Y, zl_=i % ZL)))
    loop(Y - 1, lambda i: greet(at(y_=(y + 1 + i) % Y, c_=1 - c)))
    loop(6, lambda i: greet(at(y_=group_y + i // 3, zl_=(zl + 1 + i % 3) % ZL, c_=1 - c)))
    loop(2 * (X - 1), lambda i: greet(at(x_=(x + 1 + i // 2) % X, c_=i % 2)))
    greet(at(c_=1 - c))
    for k in range(4):
        r.pair_out[2 * k : 2 * k + 2] = trunk_ref[:, k * 128 : (k + 1) * 128].astype(F32)
    pl.semaphore_wait(barrier, ZH * ZL + 5 * (Y - 1) + 6 + 2 * (X - 1))

    send(r.pair_out, r.pair_in, r.pair_s, r.pair_r, at(c_=1 - c))
    later(r.pair_s, r.pair_in)

    row_id = lax.broadcasted_iota(jnp.int32, (SEQS, tok), 0)
    pooling = (row_id == seg_ref[...]).astype(F32)
    lengths = jnp.sum(pooling, axis=1, keepdims=True)
    pooling = pooling.astype(BF16)
    row = lax.broadcasted_iota(jnp.int32, (32, 32), 0)
    col = lax.broadcasted_iota(jnp.int32, (32, 32), 1)
    place = (((row >> 2) & 3) << 3) + (((row >> 1) & 1) << 2) + ((row >> 4) << 1) + (row & 1)
    pick = (col == place).astype(F32).astype(BF16)

    wait(r.pair_r, r.pair_in)
    first = jnp.where(c == 0, r.pair_out[0:4], r.pair_in[4:8])
    second = jnp.where(c == 0, r.pair_in[0:4], r.pair_out[4:8])
    r.z_out[0:4] = first
    r.z_out[4:8] = second
    z = zh * ZL + zl

    def z_send(i):
        send(r.z_out, r.z_in.at[z], r.z_s, r.z_r.at[zh], z_peer(i)[1])

    loop(ZH * ZL - 1, z_send)
    later(r.z_s, r.z_in.at[0 : ZH * ZL - 1])
    pltpu.make_async_copy(r.z_out, r.z_in.at[z], r.z_r.at[zh]).start()

    kv_first = block * kv_tiles // 4
    kv_low, kv_high = kv_first // ZH, kv_first % ZH
    mine = c * XH + xs

    def turn(i):
        return (kv_high + i) % ZH

    def to_y(i):
        h = turn(i)
        wait(r.z_r.at[h], r.z_in.at[0:ZL])
        rows_in = r.z_in[pl.ds(h * ZL, ZL)].reshape(32, 128).astype(BF16)
        r.own[h, y] = matmul(pick, rows_in).astype(BF16).reshape(2, 16, 128)

        def one(j):
            send(r.own.at[h, y], r.own.at[h, y], r.ya_s, r.ya_r.at[h], at(y_=(y + 1 + j) % Y))

        loop(Y - 1, one)

    loop(ZH, to_y)
    later(r.ya_s, r.own.at[:, 0 : Y - 1])

    def to_x(i):
        h = turn(i)
        wait(r.ya_r.at[h], r.own.at[0, 0 : Y - 1])

        def one(j):
            send(
                r.own.at[h], r.feat.at[mine, h], r.xa_s, r.xa_r.at[mine, h],
                at(x_=(x + 1 + j) % X, c_=target_core),
            )

        loop(X - 1, one)

        @pl.when(c == target_core)
        def _():
            pltpu.make_async_copy(r.own.at[h], r.feat.at[mine, h], r.xa_r.at[mine, h]).start()

        @pl.when(c != target_core)
        def _():
            send(r.own.at[h], r.feat.at[mine, h], r.xa_s0, r.xa_r.at[mine, h], at(c_=target_core))

    loop(ZH, to_x)
    later(r.xa_s, r.feat.at[0 : X - 1])

    def settle_own():
        @pl.when(c != target_core)
        def _():
            wait(r.xa_s0, r.feat.at[0])

    pending.append(settle_own)

    same = matmul(pooling, pooling, ((0,), (0,)))
    below = lax.broadcasted_iota(jnp.int32, (tok, tok), 1) <= lax.broadcasted_iota(jnp.int32, (tok, tok), 0)
    allowed = jnp.where(below, same, 0.0) > 0.5

    def feature_tile(index):
        part = index % 4
        return r.feat[part // 2 * XH + index // (4 * ZH), index // 4 % ZH, :, part % 2].reshape(tok, 128)

    weight_copies[0].wait()
    weight_copies[1].wait()

    def query_step(i, total):
        h = turn(i)
        for src in range(X):
            if i > 0:
                wait(r.xa_r.at[src, h], r.feat.at[src, 0])
            cs, x_low = src // XH, src % XH
            start = pl.multiple_of((x_low * ZH + h) * 512 + cs * 256, 256)
            lhs = jnp.concatenate([r.feat[src, h, :, k].reshape(tok, 128) for k in range(2)], axis=1)
            total = total + matmul(lhs, r.wq[pl.ds(start, 256), :])
        return total

    for src in range(X):
        wait(r.xa_r.at[src, turn(0)], r.feat.at[src, 0])
    kv_part = jnp.zeros((tok, 256), F32)
    for k in range(kv_tiles):
        kv_part = kv_part + matmul(feature_tile(block * kv_tiles + k), r.wkv[k * 128 : (k + 1) * 128, :])
    r.kv_out[:, 0] = kv_part[:, :128].reshape(16, owned, 128)
    r.kv_out[:, 1] = kv_part[:, 128:].reshape(16, owned, 128)

    def kv_send(i):
        other, device = group_peer(i)
        send(r.kv_out.at[other], r.kv_in.at[o], r.kv_s, r.kv_r, device)

    loop(15, kv_send)
    later(r.kv_s, r.kv_in.at[0:15])
    r.kv_in[o] = r.kv_out[o]
    q_part = jnp.zeros((tok, 128), F32)
    for i in range(ZH - 1):
        q_part = query_step(i, q_part)
    wait(r.kv_r, r.kv_in.at[0:15])
    r.kv_all[o] = jnp.sum(r.kv_in[...], axis=0).reshape(2 * owned, 128).astype(BF16)

    def kv_share(i):
        send(r.kv_all.at[o], r.kv_all.at[o], r.kva_s, r.kva_r, group_peer(i)[1])

    loop(15, kv_share)
    later(r.kva_s, r.kv_all.at[0:15])
    r.q_out[...] = query_step(ZH - 1, q_part)
    send(r.q_out, r.q_in, r.q_s, r.q_r, at(c_=1 - c))
    later(r.q_s, r.q_in)

    pooled_in = matmul(pooling, feature_tile(head)) / lengths
    wait(r.q_r, r.q_in)
    queries = (r.q_out[...] + r.q_in[...]).astype(BF16)

    wait(r.kva_r, r.kv_all.at[0:15])
    kv = r.kv_all[...].astype(F32)
    keys = kv[:, :owned].reshape(tok, 128).astype(BF16)
    values = kv[:, owned:].reshape(tok, 128).astype(BF16)

    scores = matmul(queries, keys, ((1,), (1,))) * scale
    bent = jnp.tanh(scores / CAP)
    weights = jnp.where(allowed, jnp.exp(CAP * bent), 0.0)
    attention = weights / jnp.sum(weights, axis=1, keepdims=True)
    attention_low = attention.astype(BF16)
    attended = matmul(attention_low, values).astype(BF16)
    means = (matmul(pooling, attended) / lengths).astype(BF16).astype(F32)
    own_dims = jnp.where(c == 0, means[:, :64], means[:, 64:]).astype(BF16)

    weight_copies[2].wait()

    def project(side, target):
        for q in range(heads // 8):
            start = pl.multiple_of(side * (heads * 128) + q * 1024, 1024)
            piece = matmul(own_dims, r.wo[:, pl.ds(start, 1024)])
            for k in range(8):
                target[q * 8 + k] = piece[:, k * 128 : (k + 1) * 128]

    project(1 - c, r.head_out)
    send(r.head_out, r.head_in, r.h1_s, r.h1_r, at(c_=1 - c))
    later(r.h1_s, r.head_in)
    project(c, r.part_out)
    wait(r.h1_r, r.head_in)
    r.part_out[...] = r.part_out[...] + r.head_in[...]

    def part_send(i):
        other, device = head_peer(i)
        send(r.part_out.at[other], r.part_in.at[head], r.h2_s, r.h2_r, device)

    loop(heads - 1, part_send)
    later(r.h2_s, r.part_in.at[0 : heads - 1])
    r.part_in[head] = r.part_out[head]
    wait(r.h2_r, r.part_in.at[0 : heads - 1])
    r.half[head] = jnp.sum(r.part_in[...], axis=0) + pooled_in

    def half_send(i):
        send(r.half.at[head], r.half.at[head], r.h3_s, r.h3_r, head_peer(i)[1])

    loop(heads - 1, half_send)
    later(r.h3_s, r.half.at[0 : heads - 1])
    wait(r.h3_r, r.half.at[0 : heads - 1])
    send(r.half, r.hidden.at[c], r.h4_s, r.h4_r, at(c_=1 - c))
    later(r.h4_s, r.half)
    r.hidden[c] = r.half[...]
    weight_copies[3].wait()
    weight_copies[4].wait()
    gains = r.gain[...] * r.weight[...]
    wait(r.h4_r, r.half)

    hidden = jnp.concatenate([r.hidden[side, k] for side in range(2) for k in range(heads)], axis=1)
    width = tiles * 128
    squares = jnp.sum(hidden * hidden, axis=1, keepdims=True)
    weighted = jnp.sum(hidden * gains, axis=1, keepdims=True)
    rinv = lax.rsqrt(squares / width + EPS)
    rewards = rinv * weighted
    wide = jnp.broadcast_to(rewards, (SEQS, 128))
    row_id = lax.broadcasted_iota(jnp.int32, (SEQS, 128), 0)
    lane = lax.broadcasted_iota(jnp.int32, (SEQS, 128), 1)
    flat = jnp.sum(jnp.where(row_id == lane, wide, 0.0), axis=0, keepdims=True)
    reward_ref[...] = flat[:, :SEQS]
    partner = jnp.zeros((SEQS, 128), F32)
    sign = jnp.zeros((SEQS, 128), F32)
    for k in range(SEQS // 2):
        chosen, rejected = order_ref[2 * k], order_ref[2 * k + 1]
        is_chosen, is_rejected = row_id == chosen, row_id == rejected
        partner = jnp.where(is_chosen & (lane == rejected) | is_rejected & (lane == chosen), flat, partner)
        sign = jnp.where(is_chosen, -1.0, jnp.where(is_rejected, 1.0, sign))
    partner = jnp.sum(partner, axis=1, keepdims=True)
    sign = sign[:, :1]
    slope = sign * LOSS_SCALE / (1.0 + jnp.exp(sign * (partner - rewards)))
    pooled_grad = rinv * (slope * gains - hidden * (rinv * rinv * slope * weighted / width))
    dims_part = matmul(pooled_grad.astype(BF16), r.wo[...], ((1,), (1,))) / lengths
    r.dims_out[...] = jnp.concatenate([dims_part, dims_part], axis=1)
    send(r.dims_out, r.dims_in, r.d_s, r.d_r, at(c_=1 - c))
    later(r.d_s, r.dims_in)
    per_token = pooled_grad / lengths
    for k in range(tiles):
        r.token_out[k] = per_token[:, k * 128 : (k + 1) * 128]
    direct = r.token_out[c * heads + head]
    high = direct.astype(BF16)
    low = (direct - high.astype(F32)).astype(BF16)
    direct = matmul(pooling, high, ((0,), (0,))) + matmul(pooling, low, ((0,), (0,)))
    wait(r.d_r, r.dims_in)
    mine_first = (lane < 64) == (c == 0)
    mean_grad = jnp.where(mine_first, r.dims_out[...], r.dims_in[...])

    out_grad = matmul(pooling, mean_grad.astype(BF16), ((0,), (0,))).astype(BF16)
    prob_grad = matmul(out_grad, values, ((1,), (1,)))
    score_grad = attention * (prob_grad - jnp.sum(attention * prob_grad, axis=1, keepdims=True))
    raw_grad = (score_grad * (1.0 - bent * bent) * scale).astype(BF16)
    key_grad = matmul(raw_grad, queries, ((0,), (0,)))
    value_grad = matmul(attention_low, out_grad, ((0,), (0,)))
    r.dkv_out[:, 0] = key_grad.reshape(16, owned, 128)
    r.dkv_out[:, 1] = value_grad.reshape(16, owned, 128)
    own_head = ybit * ZL + zl

    def dkv_send(i):
        other = (own_head + 1 + i) % 8
        send(
            r.dkv_out.at[other // ZL * 8 + c * ZL + other % ZL], r.dkv_in.at[own_head], r.dkv_s, r.dkv_r,
            at(y_=group_y + other // ZL, zl_=other % ZL),
        )

    loop(7, dkv_send)
    later(r.dkv_s, r.dkv_in.at[0:7])
    r.dkv_in[own_head] = r.dkv_out[o]
    query_grad = matmul(raw_grad, keys).astype(BF16)

    kv_block = block * kv_tiles // 4

    def x_send(index, extra=False):
        start = pl.multiple_of(index * 512, 512)
        piece = matmul(query_grad, r.wq[pl.ds(start, 512), :], ((1,), (1,)))
        for t in range(4):
            part = piece[:, t * 128 : (t + 1) * 128]
            part = jnp.where(index * 4 + t == head, part + direct, part)
            if extra:
                part = part + r.term[t]
            r.x_out[index, :, t % 2, t // 2] = part.astype(BF16).reshape(X, rows, 128)

        def one(i):
            other = (x + 1 + i) % X
            send(r.x_out.at[index, other], r.x_in.at[index, x], r.ex_s.at[index], r.ex_r.at[index], at(x_=other))

        loop(X - 1, one)

    def y_send(index):
        wait(r.ex_r.at[index], r.x_in.at[index, 0 : X - 1])
        total = r.x_out[index, x].astype(F32)
        for i in range(X - 1):
            total = total + r.x_in[index, (x + 1 + i) % X].astype(F32)
        r.y_out[index] = total.astype(BF16)
        y_to = c * (Y // 2) + index // 2
        place = pl.ds(index % 2 * 2, 2)
        for core in range(2):
            here = (y_to == y) & (c == core)

            @pl.when(here)
            def _():
                pltpu.make_async_copy(r.y_out.at[index, core], r.y_in.at[y, place], r.ey_r.at[y]).start()

            @pl.when(jnp.logical_not(here))
            def _():
                send(
                    r.y_out.at[index, core], r.y_in.at[y, place], r.ey_s.at[index, core], r.ey_r.at[y],
                    at(y_=y_to, c_=core),
                )

    def at_turn(i):
        return (kv_block + 1 + i) % blocks

    loop(blocks - 1, lambda i: x_send(at_turn(i)))

    wait(r.dkv_r, r.dkv_in.at[0:7])
    r.dkv_all[o] = jnp.sum(r.dkv_in[...], axis=0).reshape(2 * owned, 128).astype(BF16)

    def dkv_share(i):
        send(r.dkv_all.at[o], r.dkv_all.at[o], r.dka_s, r.dka_r, group_peer(i)[1])

    loop(15, dkv_share)
    later(r.dka_s, r.dkv_all.at[0:15])
    early = blocks // 2
    loop(early, lambda i: y_send(at_turn(i)))
    wait(r.dka_r, r.dkv_all.at[0:15])
    dkv = r.dkv_all[...].astype(F32)
    dkv = jnp.concatenate([dkv[:, :owned].reshape(tok, 128), dkv[:, owned:].reshape(tok, 128)], axis=1).astype(BF16)
    kv_term = matmul(dkv, r.wkv[...], ((1,), (1,)))
    if kv_tiles < 4:
        r.term[...] = jnp.zeros_like(r.term)
    for k in range(kv_tiles):
        r.term[block * kv_tiles % 4 + k] = kv_term[:, k * 128 : (k + 1) * 128]
    x_send(kv_block, True)
    loop(blocks - early, lambda i: y_send(at_turn(early + i)))

    def settle_block(index):
        wait(r.ex_s.at[index], r.x_in.at[index, 0 : X - 1])
        for core in range(2):

            @pl.when(jnp.logical_not((c * (Y // 2) + index // 2 == y) & (c == core)))
            def _():
                wait(r.ey_s.at[index, core], r.y_out.at[index, core])

    pending.append(lambda: loop(blocks, settle_block))

    def y_wait(i):
        wait(r.ey_r.at[i], r.y_in.at[i])

    loop(Y, y_wait)
    total = r.y_in[0].astype(F32)
    for i in range(1, Y):
        total = total + r.y_in[i].astype(F32)
    for k in range(ZL):
        for h in range(ZH):
            r.l_out[h * ZL + k] = total[k, h * 8 : (h + 1) * 8]

    def l_send(i):
        other, device = z_peer(i)
        send(r.l_out.at[other], r.l_in.at[z], r.el_s, r.el_r, device)

    loop(ZH * ZL - 1, l_send)
    later(r.el_s, r.l_in.at[0 : ZH * ZL - 1])
    r.l_in[z] = r.l_out[z]
    wait(r.el_r, r.l_in.at[0 : ZH * ZL - 1])
    out_ref[...] = jnp.sum(r.l_in[...], axis=0)

    for settle in pending:
        settle()


def on_device(dims, trunk_out, segment_ids, pair_order, w_query, w_key_value, w_out, norm_gain, reward_weight):
    scratch = scratch_list(dims)
    vmem = pl.BlockSpec(memory_space=pltpu.VMEM)
    smem = pl.BlockSpec(memory_space=pltpu.SMEM)
    hbm = pl.BlockSpec(memory_space=pl.ANY)
    return pl.pallas_call(
        functools.partial(kernel, dims, tuple(scratch)),
        out_shape=(jax.ShapeDtypeStruct((8, 128), F32), jax.ShapeDtypeStruct((1, SEQS), F32)),
        in_specs=[vmem, vmem, smem] + [hbm] * 5,
        out_specs=(vmem, vmem),
        scratch_shapes=tuple(scratch.values()),
        compiler_params=pltpu.CompilerParams(
            collective_id=0, has_side_effects=True, vmem_limit_bytes=63 * 1024 * 1024
        ),
    )(
        trunk_out, segment_ids.reshape(1, -1), pair_order, w_query[0, 0], w_key_value[0, 0], w_out[0], norm_gain,
        reward_weight,
    )


def solution(mesh):
    members, shards = mesh.shape["member"], mesh.shape["shard"]
    z_high = 4 if members > 4 else 2
    dims = (members // z_high, z_high, shards // (2 * ZL))
    placed = (
        P("shard", "member"),
        P(),
        P(),
        P("member", "shard", None, None),
        P("member", "shard", None, None),
        P("member", "shard", None),
        P("member", None),
        P("member", None),
    )
    return jax.shard_map(
        functools.partial(on_device, dims),
        mesh=mesh,
        in_specs=placed,
        out_specs=(P("member", "shard"), P("member", None)),
        check_vma=False,
    )
```
